256 devices in a mesh: ctx: 16 (over x, y_hi, core), head: 16 (over y_lo, z).
Axes of the slice: x: 4, y: 4 (y_hi: 2, y_lo: 2; y = y_hi * 2 + y_lo), z: 8, core: 2. Of those that a mesh axis runs over, the one named last changes fastest.
Arguments:
- queries: bfloat16 [8192, 7168], P(('ctx', 'head')), may hold values from -120 to 120, as said below
- keys: bfloat16 [8192, 1024], P(('ctx', 'head')), may hold values from -5 to 5, as said below
- values: bfloat16 [8192, 1024], P(('ctx', 'head')), may hold values from -6 to 6
- order: int32 [32], replicated, may hold values from 0 to 31, each once
Outputs:
- attended: bfloat16 [8192, 7168], P(('ctx', 'head'))
The draws below stay inside these ranges and needn't reach their ends.
Inputs may be any that keep to these rules, and one draw needn't show every extreme that they name: `queries`: each query row lies within the bound. `keys`: each key entry lies within the bound.
All inputs are finite; a program needn't handle non-finite values.
Results may differ from the reference program's by a relative error of at most 0.006.
Values may be sent and summed in bfloat16 or wider, within the bound.
A program may use at most 128 MiB of HBM per device.

```python
import math
import jax
import jax.numpy as jnp
from jax import lax

HD = 128
QH = 56
KVH = 8
BLK = 256
BLOCKS = 32
SEQ = 8192


def paired_rows(key, boost):
    key_part, query_part = jax.random.split(key, 2)
    key_rows = jnp.clip(jax.random.normal(key_part, (SEQ, KVH * HD), jnp.float32), -5.0, 5.0)
    query_rows = jnp.clip(jax.random.normal(query_part, (SEQ, QH * HD), jnp.float32), -6.0, 6.0)
    rows = jnp.arange(SEQ)
    focus = (rows % BLK == BLK // 2).astype(jnp.float32)[:, None] * boost
    before = (rows % BLK == BLK // 2 - 1).astype(jnp.float32)[:, None] * boost
    query_rows = (1.0 - focus) * query_rows
    key_rows = (1.0 - before) * key_rows
    return (query_rows, key_rows)


def draw_queries(key, part):
    boost = 0.0
    query_rows, key_rows = paired_rows(key, boost)
    return query_rows.astype(jnp.bfloat16)


def draw_keys(key, part):
    boost = 0.0
    query_rows, key_rows = paired_rows(key, boost)
    return key_rows.astype(jnp.bfloat16)


def steps_of(key, dims, shards, low, top_value):
    factor_of, own = 1.0, jax.random.fold_in(key, 6)
    for axis_at, blocks in shards:
        steps = jnp.exp(jax.random.uniform(jax.random.fold_in(own, axis_at), (blocks,), jnp.float32, low / len(shards), top_value / len(shards)))
        factor_of = factor_of * jnp.repeat(steps, dims[axis_at] // blocks).reshape([-1 if axis == axis_at else 1 for axis in range(len(dims))])
    return factor_of


def centred(key, extent, width, limit, cuts=(), held_as=jnp.bfloat16):
    drawn = jax.random.normal(key, extent, jnp.float32) * width
    if len(cuts) > 0:
        drawn = steps_of(key, extent, cuts, -0.22, 0.18) * drawn
    return jnp.clip(drawn, min=-limit, max=limit).astype(held_as)


def setup_inputs(seed: int = 0) -> dict:
    streams_of = jax.random.split(jax.random.key(seed), 5)
    queries = draw_queries(jax.random.fold_in(streams_of[4], 71), 0)
    keys = draw_keys(jax.random.fold_in(streams_of[4], 71), 0)
    values = centred(streams_of[2], (SEQ, KVH * HD), 1.0, 6.0, ((0, 256),))
    order = jax.random.permutation(streams_of[3], BLOCKS).astype(jnp.int32)
    return dict(queries=queries, keys=keys, values=values, order=order)


def reference(queries, keys, values, order):
    rows = jnp.arange(SEQ, dtype=jnp.int32)
    position = order[rows // BLK] * BLK + rows % BLK
    query_block = math.gcd(1024, SEQ)
    count = SEQ // query_block
    group = QH // KVH
    scale = HD ** -0.5

    def one_head(head_index):
        kv_index = head_index // group
        query_cols = lax.dynamic_slice_in_dim(queries, (head_index * HD).astype(jnp.int32), HD, 1)
        key_cols = lax.dynamic_slice_in_dim(keys, (kv_index * HD).astype(jnp.int32), HD, 1)
        value_cols = lax.dynamic_slice_in_dim(values, (kv_index * HD).astype(jnp.int32), HD, 1)

        def one_block(block_index):
            begin = (block_index * query_block).astype(jnp.int32)
            query_rows = lax.dynamic_slice_in_dim(query_cols, begin, query_block, 0)
            query_pos = lax.dynamic_slice_in_dim(position, begin, query_block, 0)
            score = jnp.dot(query_rows, key_cols.T, preferred_element_type=jnp.float32) * scale
            kept = position[None, :] <= query_pos[:, None]
            top = jnp.max(jnp.where(kept, score, -jnp.inf), axis=1, keepdims=True)
            weight = jnp.where(kept, jnp.exp(score - top), 0.0)
            total = jnp.sum(weight, axis=1, keepdims=True)
            mixed = jnp.dot(weight.astype(jnp.bfloat16), value_cols, preferred_element_type=jnp.float32)
            return (mixed / total).astype(jnp.bfloat16)

        return lax.map(one_block, jnp.arange(count, dtype=jnp.int32)).reshape(SEQ, HD)

    result = lax.map(one_head, jnp.arange(QH, dtype=jnp.int32))
    return jnp.transpose(result, (1, 0, 2)).reshape(SEQ, QH * HD)
```

```python
import jax
import jax.numpy as jnp
from jax import lax
from jax.experimental import pallas as pl
from jax.experimental.pallas import tpu as pltpu
from jax.sharding import PartitionSpec as P

MESH = pl.DeviceIdType.MESH
HD = 128
GROUP = 7
PLANES = 8
BLOCKS = 32
PART = 32
ROWS = 8
BLK = 256
QROWS = GROUP * ROWS
QALL = BLOCKS * QROWS
CHUNK = BLOCKS * PART
WIDE = GROUP * HD
TILE = 256
TILES = QALL // TILE
VROWS = HD + 16
SCALE = HD**-0.5 * 1.4426950408889634
LOW = -1e30

SPAN = [
    ((TILE * t) // QROWS * PART, ((TILE * t + TILE - 1) // QROWS + 1) * PART) for t in range(TILES)
]
EDGE = max(last - first for first, last in SPAN)


def kernel(
    order, block_at, q_in, k_in, v_in, out,
    q_buf, raw, kv, qs, ones, acc, top, bias, result, o_buf,
    q_send, q_recv, q_own, kv_send, kv_recv, kv_own,
    up_send, up_recv, down_send, down_recv, near_send, near_recv,
    o_send, o_recv, o_own,
):
    ctx = lax.axis_index("ctx")
    head = lax.axis_index("head")
    z = lax.rem(head, PLANES)
    y_lo = head // PLANES
    core = lax.rem(ctx, 2)
    g = ctx // 2
    part = 2 * y_lo + core
    me = 2 * ctx + y_lo
    sibling = (ctx + 1 - 2 * core, head)
    above = (ctx, y_lo * PLANES + lax.rem(z + 1, PLANES))
    below = (ctx, y_lo * PLANES + lax.rem(z + PLANES - 1, PLANES))

    def plane_device(index):
        return (index // 2, lax.rem(index, 2) * PLANES + z)

    barrier = pltpu.get_barrier_semaphore()

    def greet(i, carry):
        pl.semaphore_signal(
            barrier, inc=1, device_id=plane_device(lax.rem(me + i, 32)), device_id_type=MESH
        )
        return carry

    lax.fori_loop(1, 32, greet, 0)
    for device in (above, below):
        pl.semaphore_signal(barrier, inc=1, device_id=device, device_id_type=MESH)

    own_q = pltpu.make_async_copy(
        q_in.at[part, :, pl.ds(pl.multiple_of(g * WIDE, HD), WIDE)], q_buf.at[me], q_own
    )
    own_q.start()

    def for_core(of, do):
        for which, source in ((0, k_in), (1, v_in)):
            pl.when(of == which)(lambda source=source: do(source))

    own_columns = pl.ds(pl.multiple_of(g * HD, HD), HD)
    for_core(
        core, lambda source: pltpu.make_async_copy(source.at[:, own_columns], raw.at[me], kv_own).start()
    )

    pl.semaphore_wait(barrier, 33)

    def send_kv(i, carry):
        target = lax.rem(me + i, 32)
        to_ctx, to_y = target // 2, lax.rem(target, 2)
        columns = pl.ds(pl.multiple_of(to_ctx // 2 * HD, HD), HD)
        for_core(
            lax.rem(to_ctx, 2),
            lambda source: pltpu.make_async_remote_copy(
                src_ref=source.at[:, columns], dst_ref=raw.at[me],
                send_sem=kv_send, recv_sem=kv_recv,
                device_id=(to_ctx, to_y * PLANES + z), device_id_type=MESH,
            ).start(),
        )
        return carry

    lax.fori_loop(1, 32, send_kv, 0)

    def send_q(i, carry):
        target = lax.rem(me + i, 32)
        to_ctx, to_y = target // 2, lax.rem(target, 2)
        columns = pl.ds(pl.multiple_of(to_ctx // 2 * WIDE, HD), WIDE)
        pltpu.make_async_remote_copy(
            src_ref=q_in.at[2 * to_y + lax.rem(to_ctx, 2), :, columns],
            dst_ref=q_buf.at[me],
            send_sem=q_send,
            recv_sem=q_recv,
            device_id=(to_ctx, to_y * PLANES + z),
            device_id_type=MESH,
        ).start()
        return carry

    lax.fori_loop(1, 32, send_q, 0)

    def ring(distance, upward):
        if upward:
            chunk, device, sems = lax.rem(z + PLANES - (distance - 1), PLANES), above, (up_send, up_recv)
        else:
            chunk, device, sems = lax.rem(z + distance - 1, PLANES), below, (down_send, down_recv)
        whole = kv.at[chunk, core]
        if distance == 4:
            whole = whole.at[pl.ds(0 if upward else CHUNK // 2, CHUNK // 2)]
        return pltpu.make_async_remote_copy(
            src_ref=whole, dst_ref=whole,
            send_sem=sems[0].at[distance - 1], recv_sem=sems[1].at[distance - 1],
            device_id=device, device_id_type=MESH,
        )

    def across(step, chunk):
        return pltpu.make_async_remote_copy(
            src_ref=kv.at[chunk, core], dst_ref=kv.at[chunk, core],
            send_sem=near_send.at[step], recv_sem=near_recv.at[step],
            device_id=sibling, device_id_type=MESH,
        )

    for t, (first, last) in enumerate(SPAN):
        shape = (last - first, TILE)
        row = lax.broadcasted_iota(jnp.int32, shape, 0) + first
        column = lax.broadcasted_iota(jnp.int32, shape, 1) + t * TILE
        key_block, query_block = row // PART, column // QROWS
        key_row, query_row = lax.rem(row, PART), lax.rem(column, ROWS)
        mine = z * PART + part * ROWS + query_row
        for kind, (key_at, query_at) in enumerate(
            ((0, 0), (z * PART + key_row, mine), (1, 0))
        ):
            kept = key_block * BLK + key_at <= query_block * BLK + query_at
            bias[kind, t, : last - first, :] = jnp.where(kept, 0.0, LOW)
    ones[...] = jnp.ones_like(ones)
    acc[...] = jnp.zeros_like(acc)
    top[...] = jnp.full_like(top, LOW)

    pltpu.make_async_copy(raw.at[0], raw.at[0], kv_own).wait()
    many = raw.at[pl.ds(0, 31)]
    pltpu.make_async_copy(many, many, kv_recv).wait()
    for p in range(0, BLOCKS, 4):
        rows = jnp.concatenate([raw[block_at[p + i]] for i in range(4)], axis=0)

        @pl.when(core == 0)
        def _():
            kv[z, 0, p * PART : (p + 4) * PART, :] = rows

        @pl.when(core == 1)
        def _():
            kv[z, 1, p * PART : (p + 4) * PART, :] = rows.T

    ring(1, True).start()
    ring(1, False).start()
    across(0, z).start()

    own_q.wait()
    many_q = q_buf.at[pl.ds(0, 31)]
    pltpu.make_async_copy(many_q, many_q, q_recv).wait()

    def heads_as_rows(block):
        return jnp.concatenate([block[:, j * HD : (j + 1) * HD] for j in range(GROUP)], axis=0)

    for p in range(0, BLOCKS, 2):
        pair = [heads_as_rows(q_buf[block_at[p + i]]) for i in range(2)]
        qs[p * QROWS : (p + 2) * QROWS, :] = jnp.concatenate(pair, axis=0)

    def one_chunk(step, carry):
        distance = (step + 1) // 2
        from_below = lax.rem(step, 2) == 1
        chunk = lax.rem(jnp.where(from_below, z + PLANES - distance, z + distance), PLANES)
        for d in range(1, 5):

            @pl.when(step == 2 * d - 1)
            def _():
                ring(d, True).wait_recv()
                ring(d, False).wait_recv()
                if d < 4:
                    ring(d + 1, True).start()
                    ring(d + 1, False).start()
                    across(2 * d - 1, lax.rem(z + PLANES - d, PLANES)).start()
                    across(2 * d, lax.rem(z + d, PLANES)).start()
                else:
                    across(7, lax.rem(z + 4, PLANES)).start()

        other = kv.at[chunk, 1 - core]
        pltpu.make_async_copy(other, other, near_recv.at[step]).wait()

        kind = jnp.where(chunk < z, 0, jnp.where(chunk == z, 1, 2))
        def scores(t):
            return lax.dot_general(
                kv[chunk, 0, : SPAN[t][1], :], qs[t * TILE : (t + 1) * TILE, :],
                (((1,), (1,)), ((), ())), preferred_element_type=jnp.float32,
            )

        def weights(t, score):
            first, last = SPAN[t]
            edge = score[first:] + bias[kind, t, : last - first, :]
            score = jnp.concatenate([score[:first], edge], axis=0) if first else edge
            old = top[t]
            here = jnp.max(jnp.max(score.reshape(last // 8, 8, TILE), axis=0), axis=0, keepdims=True)
            new = jnp.maximum(old, jnp.broadcast_to(here, (8, TILE)))
            top[t] = new
            weight = jnp.exp2((score - new[0:1]) * SCALE).astype(jnp.bfloat16)
            return weight, jnp.exp2((old - new) * SCALE)

        def add(t, weight, factor):
            last = SPAN[t][1]
            values = [kv[chunk, 1, at : at + HD, : min(HD, last - at)] for at in range(0, last, HD)]
            columns = jnp.concatenate([jnp.concatenate(values, axis=1), ones[:, :last]], axis=0)
            mixed = jnp.dot(columns, weight, preferred_element_type=jnp.float32)
            acc[t] = acc[t] * factor[0:1] + mixed

        score, before = scores(0), None
        for t in range(TILES):
            following = scores(t + 1) if t + 1 < TILES else None
            current = (t,) + weights(t, score)
            if before is not None:
                add(*before)
            before, score = current, following
        add(*before)
        return carry

    lax.fori_loop(0, PLANES, one_chunk, 0)

    for t in range(TILES):
        total = acc[t]
        rows = (total[:HD] / total[HD : HD + 1]).T
        at = t * TILE
        while at < (t + 1) * TILE:
            block, row = at // QROWS, at % QROWS
            count = min(QROWS - row, (t + 1) * TILE - at)
            result[block, row : row + count, :] = rows[at - t * TILE : at - t * TILE + count]
            at += count

    def out_copy(b, device_rows):
        return out.at[device_rows, :, pl.ds(pl.multiple_of(g * WIDE, HD), WIDE)]

    def send_back(i, carry):
        b = lax.rem(me + i, BLOCKS)
        rows = result[order[b]].astype(jnp.bfloat16)
        o_buf[b] = jnp.concatenate([rows[j * ROWS : (j + 1) * ROWS] for j in range(GROUP)], axis=1)

        @pl.when(i < BLOCKS)
        def _():
            pltpu.make_async_remote_copy(
                src_ref=o_buf.at[b], dst_ref=out_copy(b, part),
                send_sem=o_send, recv_sem=o_recv,
                device_id=plane_device(b), device_id_type=MESH,
            ).start()

        return carry

    lax.fori_loop(1, BLOCKS + 1, send_back, 0)
    own_o = pltpu.make_async_copy(o_buf.at[me], out_copy(me, part), o_own)
    own_o.start()

    many_o = o_buf.at[pl.ds(0, 31)]
    pltpu.make_async_copy(many_q, many_q, q_send).wait()
    pltpu.make_async_copy(many, many, kv_send).wait()
    for d in range(1, 5):
        ring(d, True).wait_send()
        ring(d, False).wait_send()
    for step in range(PLANES):
        across(step, z).wait_send()
    own_o.wait()
    pltpu.make_async_copy(many_o, many_o, o_send).wait()
    pltpu.make_async_copy(many_o, many_o, o_recv).wait()


def shards(queries, keys, values, order):
    stored = jnp.arange(BLOCKS, dtype=jnp.int32)
    block_at = jnp.sum(jnp.where(order[None, :] == stored[:, None], stored[None, :], 0), axis=1)
    hbm = pl.BlockSpec(memory_space=pl.ANY)
    dma = pltpu.SemaphoreType.DMA
    out = pl.pallas_call(
        kernel,
        out_shape=jax.ShapeDtypeStruct((PART // ROWS, ROWS, 8 * WIDE), jnp.bfloat16),
        in_specs=[pl.BlockSpec(memory_space=pltpu.SMEM)] * 2 + [hbm, hbm, hbm],
        out_specs=hbm,
        scratch_shapes=[
            pltpu.VMEM((BLOCKS, ROWS, WIDE), jnp.bfloat16),
            pltpu.VMEM((BLOCKS, PART, HD), jnp.bfloat16),
            pltpu.VMEM((PLANES, 2, CHUNK, HD), jnp.bfloat16),
            pltpu.VMEM((QALL, HD), jnp.bfloat16),
            pltpu.VMEM((VROWS - HD, CHUNK), jnp.bfloat16),
            pltpu.VMEM((TILES, VROWS, TILE), jnp.float32),
            pltpu.VMEM((TILES, 8, TILE), jnp.float32),
            pltpu.VMEM((3, TILES, EDGE, TILE), jnp.float32),
            pltpu.VMEM((BLOCKS, QROWS, HD), jnp.float32),
            pltpu.VMEM((BLOCKS, ROWS, WIDE), jnp.bfloat16),
            dma, dma, dma, dma, dma, dma,
            dma((4,)), dma((4,)), dma((4,)), dma((4,)), dma((8,)), dma((8,)),
            dma, dma, dma,
        ],
        compiler_params=pltpu.CompilerParams(
            collective_id=0, has_side_effects=True, vmem_limit_bytes=48 * 2**20
        ),
        cost_estimate=pl.CostEstimate(
            flops=4 * QALL * BLOCKS * BLK * HD // 2, bytes_accessed=2**21, transcendentals=QALL * 4096
        ),
    )(order, block_at, queries.reshape(PART // ROWS, ROWS, 8 * WIDE), keys, values)
    return out.reshape(PART, 8 * WIDE)


def solution(mesh):
    rows = P(("ctx", "head"), None)
    return jax.shard_map(
        shards, mesh=mesh, in_specs=(rows, rows, rows, P()), out_specs=rows, check_vma=False
    )
```

```python
import jax
import jax.numpy as jnp
from jax import lax
from jax.experimental import pallas as pl
from jax.experimental.pallas import tpu as pltpu
from jax.sharding import PartitionSpec as P

MESH = pl.DeviceIdType.MESH
HD = 128
GROUP = 7
PLANES = 8
BLOCKS = 32
PART = 32
ROWS = 8
BLK = 256
QROWS = GROUP * ROWS
QALL = BLOCKS * QROWS
CHUNK = BLOCKS * PART
WIDE = GROUP * HD
TILE = 256
TILES = QALL // TILE
VROWS = HD + 16
SCALE = HD**-0.5 * 1.4426950408889634
MASKED = -1e30

SPAN = [
    ((TILE * t) // QROWS * PART, ((TILE * t + TILE - 1) // QROWS + 1) * PART) for t in range(TILES)
]
EDGE = max(last - first for first, last in SPAN)

PIECES = 4
PIECE = CHUNK // PIECES
UP, DOWN = (0, 1, 2, 3), (1, 0, 3, 2)
HALF = CHUNK // 2
LOW = [(t, 0, min(HALF, last)) for t, (first, last) in enumerate(SPAN)]
HIGH = [(t, HALF, last) for t, (first, last) in enumerate(SPAN) if last > HALF]


def kernel(
    order, q_in, k_in, v_in, out,
    q_held, kv_in, kv_held, q_buf, raw, kv, qs, ones, acc, top, bias, result, o_buf, block_at,
    fetch, q_send, q_recv, q_own, kv_send, kv_recv, kv_own,
    up_send, up_recv, down_send, down_recv, near_send, near_recv,
    o_send, o_recv, o_own,
):
    ctx = lax.axis_index("ctx")
    head = lax.axis_index("head")
    z = lax.rem(head, PLANES)
    y_lo = head // PLANES
    core = lax.rem(ctx, 2)
    g = ctx // 2
    part = 2 * y_lo + core
    me = 2 * ctx + y_lo
    sibling = (ctx + 1 - 2 * core, head)
    above = (ctx, y_lo * PLANES + lax.rem(z + 1, PLANES))
    below = (ctx, y_lo * PLANES + lax.rem(z + PLANES - 1, PLANES))

    def plane_device(index):
        return (index // 2, lax.rem(index, 2) * PLANES + z)

    fetches = [
        pltpu.make_async_copy(k_in, kv_in.at[0], fetch.at[0]),
        pltpu.make_async_copy(v_in, kv_in.at[1], fetch.at[1]),
        pltpu.make_async_copy(q_in, q_held, fetch.at[2]),
    ]
    for copy in fetches:
        copy.start()

    barrier = pltpu.get_barrier_semaphore()

    def greet(i, carry):
        pl.semaphore_signal(
            barrier, inc=1, device_id=plane_device(lax.rem(me + i, 32)), device_id_type=MESH
        )
        return carry

    lax.fori_loop(1, 32, greet, 0)
    for device in (above, below):
        pl.semaphore_signal(barrier, inc=1, device_id=device, device_id_type=MESH)

    fetches[0].wait()
    fetches[1].wait()
    for which in range(2):
        for to_g in range(8):
            kv_held[which, to_g] = kv_in[which, :, to_g * HD : (to_g + 1) * HD]
    own_kv = pltpu.make_async_copy(kv_held.at[core, g], raw.at[me], kv_own)
    own_kv.start()

    pl.semaphore_wait(barrier, 33)

    def send_kv(i, carry):
        target = lax.rem(me + i, 32)
        to_ctx, to_y = target // 2, lax.rem(target, 2)
        pltpu.make_async_remote_copy(
            src_ref=kv_held.at[lax.rem(to_ctx, 2), to_ctx // 2], dst_ref=raw.at[me],
            send_sem=kv_send, recv_sem=kv_recv,
            device_id=(to_ctx, to_y * PLANES + z), device_id_type=MESH,
        ).start()
        return carry

    lax.fori_loop(1, 32, send_kv, 0)

    fetches[2].wait()
    own_q = pltpu.make_async_copy(
        q_held.at[part, :, pl.ds(pl.multiple_of(g * WIDE, HD), WIDE)], q_buf.at[me], q_own
    )
    own_q.start()

    def send_q(i, carry):
        target = lax.rem(me + i, 32)
        to_ctx, to_y = target // 2, lax.rem(target, 2)
        columns = pl.ds(pl.multiple_of(to_ctx // 2 * WIDE, HD), WIDE)
        pltpu.make_async_remote_copy(
            src_ref=q_held.at[2 * to_y + lax.rem(to_ctx, 2), :, columns],
            dst_ref=q_buf.at[me],
            send_sem=q_send,
            recv_sem=q_recv,
            device_id=(to_ctx, to_y * PLANES + z),
            device_id_type=MESH,
        ).start()
        return carry

    lax.fori_loop(1, 32, send_q, 0)

    def ring(distance, upward, turn):
        if upward:
            chunk, device, sems = lax.rem(z + PLANES + 1 - distance, PLANES), above, (up_send, up_recv)
        else:
            chunk, device, sems = lax.rem(z + distance - 1, PLANES), below, (down_send, down_recv)
        held = kv.at[chunk, core, pl.ds((UP if upward else DOWN)[turn] * PIECE, PIECE)]
        index = (distance - 1) * PIECES + turn
        return pltpu.make_async_remote_copy(
            src_ref=held, dst_ref=held,
            send_sem=sems[0].at[index], recv_sem=sems[1].at[index],
            device_id=device, device_id_type=MESH,
        )

    def across(step, chunk, first, count=1):
        held = kv.at[chunk, core, pl.ds(first * PIECE, count * PIECE)]
        return pltpu.make_async_remote_copy(
            src_ref=held, dst_ref=held,
            send_sem=near_send.at[step], recv_sem=near_recv.at[step],
            device_id=sibling, device_id_type=MESH,
        )

    def pass_on(distance, turn):
        ring(distance, True, turn).wait_recv()
        ring(distance, False, turn).wait_recv()

        @pl.when((distance < 3) | (distance == 3) & (turn % 2 == 0))
        def _():
            ring(distance + 1, True, turn).start()
            ring(distance + 1, False, turn).start()

        step = 2 * distance + turn // 2
        across(step, lax.rem(z + PLANES - distance, PLANES), UP[turn]).start()
        across(step, lax.rem(z + distance, PLANES), DOWN[turn]).start()

    def from_sibling(step, count):
        held = kv.at[z, 1 - core, pl.ds(0, count * PIECE)]
        pltpu.make_async_copy(held, held, near_recv.at[step]).wait()

    for p in range(BLOCKS):
        at = jnp.int32(0)
        for b in range(BLOCKS):
            at = at + jnp.where(order[b] == p, b, 0)
        block_at[p] = jnp.minimum(at, BLOCKS - 1)
    for t, (first, last) in enumerate(SPAN):
        shape = (last - first, TILE)
        row = lax.broadcasted_iota(jnp.int32, shape, 0) + first
        column = lax.broadcasted_iota(jnp.int32, shape, 1) + t * TILE
        key_block, query_block = row // PART, column // QROWS
        key_row, query_row = lax.rem(row, PART), lax.rem(column, ROWS)
        mine = z * PART + part * ROWS + query_row
        for kind, (key_at, query_at) in enumerate(
            ((0, 0), (z * PART + key_row, mine), (1, 0))
        ):
            kept = key_block * BLK + key_at <= query_block * BLK + query_at
            bias[kind, t, : last - first, :] = jnp.where(kept, 0.0, MASKED)
    ones[...] = jnp.ones_like(ones)
    acc[...] = jnp.zeros_like(acc)
    top[...] = jnp.full_like(top, MASKED)

    own_kv.wait()
    many = raw.at[pl.ds(0, 31)]
    pltpu.make_async_copy(many, many, kv_recv).wait()
    def sort_piece(piece):
        for p in range(piece * 8, piece * 8 + 8, 4):
            rows = jnp.concatenate([raw[block_at[p + i]] for i in range(4)], axis=0)

            @pl.when(core == 0)
            def _():
                kv[z, 0, p * PART : (p + 4) * PART, :] = rows

            @pl.when(core == 1)
            def _():
                kv[z, 1, p * PART : (p + 4) * PART, :] = rows.T

        across(piece // 2, z, piece).start()

    sort_piece(0)
    ring(1, True, 0).start()
    sort_piece(1)
    ring(1, False, 0).start()
    ring(1, True, 1).start()
    ring(1, False, 1).start()
    sort_piece(2)
    ring(1, True, 2).start()
    sort_piece(3)
    ring(1, False, 2).start()
    ring(1, True, 3).start()
    ring(1, False, 3).start()

    pass_on(1, 0)
    from_sibling(0, 2)
    own_q.wait()
    many_q = q_buf.at[pl.ds(0, 31)]
    pltpu.make_async_copy(many_q, many_q, q_recv).wait()

    def heads_as_rows(block):
        return jnp.concatenate([block[:, j * HD : (j + 1) * HD] for j in range(GROUP)], axis=0)

    for p in range(0, BLOCKS, 2):
        pair = [heads_as_rows(q_buf[block_at[p + i]]) for i in range(2)]
        qs[p * QROWS : (p + 2) * QROWS, :] = jnp.concatenate(pair, axis=0)

    def attend(chunks, between):
        spans = LOW + HIGH
        kinds = [jnp.where(chunk < z, 0, jnp.where(chunk == z, 1, 2)) for chunk in chunks]

        def scores(span):
            t, begin, end = span
            held = [kv[chunk, 0, begin:end, :] for chunk in chunks]
            held = jnp.concatenate(held, axis=0) if len(held) > 1 else held[0]
            return lax.dot_general(
                held, qs[t * TILE : (t + 1) * TILE, :],
                (((1,), (1,)), ((), ())), preferred_element_type=jnp.float32,
            )

        def weights(span, score):
            t, begin, end = span
            edge = max(SPAN[t][0], begin)
            parts = []
            for i, kind in enumerate(kinds):
                part = score[i * (end - begin) : (i + 1) * (end - begin)]
                if edge >= end:
                    parts.append(part)
                    continue
                if edge > begin:
                    parts.append(part[: edge - begin])
                parts.append(part[edge - begin :] + bias[kind, t, edge - SPAN[t][0] : end - SPAN[t][0], :])
            score = jnp.concatenate(parts, axis=0) if len(parts) > 1 else parts[0]
            old = top[t]
            here = jnp.max(score.reshape(score.shape[0] // 8, 8, TILE), axis=0)
            here = jnp.max(here, axis=0, keepdims=True)
            new = jnp.maximum(old, jnp.broadcast_to(here, (8, TILE)))
            top[t] = new
            weight = jnp.exp2((score - new[0:1]) * SCALE).astype(jnp.bfloat16)
            return weight, jnp.exp2((old - new) * SCALE)

        def add(span, weight, factor):
            t, begin, end = span
            values = [
                kv[chunk, 1, at : at + HD, : min(HD, end - at)]
                for chunk in chunks for at in range(begin, end, HD)
            ]
            columns = jnp.concatenate(values, axis=1) if len(values) > 1 else values[0]
            columns = jnp.concatenate([columns, ones[:, : weight.shape[0]]], axis=0)
            acc[t] = acc[t] * factor[0:1] + jnp.dot(columns, weight, preferred_element_type=jnp.float32)

        score, before = scores(spans[0]), None
        for i, span in enumerate(spans):
            following = scores(spans[i + 1]) if i + 1 < len(spans) else None
            current = (span,) + weights(span, score)
            if before is not None:
                add(*before)
            before, score = current, following
            if i in between:
                between[i]()
        add(*before)

    def one_distance(distance, carry):
        lower, upper = lax.rem(z + PLANES - distance, PLANES), lax.rem(z + distance, PLANES)
        alone = (distance == 0) | (distance == 4)

        @pl.when(alone)
        def _():
            def late_first():
                pl.when(distance == 0)(lambda: pass_on(1, 1))

            def late_high():
                @pl.when(distance == 0)
                def _():
                    from_sibling(1, 2)

                @pl.when(distance == 4)
                def _():
                    pass_on(4, 2)
                    from_sibling(9, 2)

            attend((upper,), {1: late_first, len(LOW) - 2: late_high})
            pl.when(distance == 0)(lambda: from_sibling(2, 4))

        @pl.when(jnp.logical_not(alone))
        def _():
            def last_piece():
                pass_on(distance, 3)
                from_sibling(2 * distance + 1, 4)

            def next_second():
                pl.when(distance < 3)(lambda: pass_on(distance + 1, 1))

            attend(
                (lower, upper),
                {
                    2: lambda: pass_on(distance, 2),
                    len(LOW) - 2: last_piece,
                    len(LOW) + 1: lambda: pass_on(distance + 1, 0),
                    len(LOW) + 2: next_second,
                },
            )
            pl.when(distance < 3)(lambda: from_sibling(2 * distance + 2, 4))
            pl.when(distance == 3)(lambda: from_sibling(8, 2))

        return carry

    lax.fori_loop(0, 5, one_distance, 0)

    for t in range(TILES):
        total = acc[t]
        rows = (total[:HD] / total[HD : HD + 1]).T
        at = t * TILE
        while at < (t + 1) * TILE:
            block, row = at // QROWS, at % QROWS
            count = min(QROWS - row, (t + 1) * TILE - at)
            result[block, row : row + count, :] = rows[at - t * TILE : at - t * TILE + count]
            at += count

    def out_copy(b, device_rows):
        return out.at[device_rows, :, pl.ds(pl.multiple_of(g * WIDE, HD), WIDE)]

    def send_back(i, carry):
        b = lax.rem(me + i, BLOCKS)
        rows = result[order[b]].astype(jnp.bfloat16)
        o_buf[b] = jnp.concatenate([rows[j * ROWS : (j + 1) * ROWS] for j in range(GROUP)], axis=1)

        @pl.when(i < BLOCKS)
        def _():
            pltpu.make_async_remote_copy(
                src_ref=o_buf.at[b], dst_ref=out_copy(b, part),
                send_sem=o_send, recv_sem=o_recv,
                device_id=plane_device(b), device_id_type=MESH,
            ).start()

        return carry

    lax.fori_loop(1, BLOCKS + 1, send_back, 0)
    own_o = pltpu.make_async_copy(o_buf.at[me], out_copy(me, part), o_own)
    own_o.start()

    many_o = o_buf.at[pl.ds(0, 31)]
    pltpu.make_async_copy(many_q, many_q, q_send).wait()
    pltpu.make_async_copy(many, many, kv_send).wait()
    for distance in range(1, 5):
        for turn in range(0, PIECES, 1 if distance < 4 else 2):
            ring(distance, True, turn).wait_send()
            ring(distance, False, turn).wait_send()
    for step in range(10):
        across(step, z, 0, 4 if 2 <= step < 8 else 2).wait_send()
    own_o.wait()
    pltpu.make_async_copy(many_o, many_o, o_send).wait()
    pltpu.make_async_copy(many_o, many_o, o_recv).wait()


def shards(queries, keys, values, order):
    hbm = pl.BlockSpec(memory_space=pltpu.HBM)
    dma = pltpu.SemaphoreType.DMA
    out = pl.pallas_call(
        kernel,
        out_shape=pltpu.VMEM((PART // ROWS, ROWS, 8 * WIDE), jnp.bfloat16),
        in_specs=[pl.BlockSpec(memory_space=pltpu.SMEM), hbm, hbm, hbm],
        out_specs=pl.BlockSpec(memory_space=pltpu.VMEM),
        scratch_shapes=[
            pltpu.VMEM((PART // ROWS, ROWS, 8 * WIDE), jnp.bfloat16),
            pltpu.VMEM((2, PART, 8 * HD), jnp.bfloat16),
            pltpu.VMEM((2, 8, PART, HD), jnp.bfloat16),
            pltpu.VMEM((BLOCKS, ROWS, WIDE), jnp.bfloat16),
            pltpu.VMEM((BLOCKS, PART, HD), jnp.bfloat16),
            pltpu.VMEM((PLANES, 2, CHUNK, HD), jnp.bfloat16),
            pltpu.VMEM((QALL, HD), jnp.bfloat16),
            pltpu.VMEM((VROWS - HD, CHUNK), jnp.bfloat16),
            pltpu.VMEM((TILES, VROWS, TILE), jnp.float32),
            pltpu.VMEM((TILES, 8, TILE), jnp.float32),
            pltpu.VMEM((3, TILES, EDGE, TILE), jnp.float32),
            pltpu.VMEM((BLOCKS, QROWS, HD), jnp.float32),
            pltpu.VMEM((BLOCKS, ROWS, WIDE), jnp.bfloat16),
            pltpu.SMEM((BLOCKS,), jnp.int32),
            dma((3,)), dma, dma, dma, dma, dma, dma,
            *[dma((4 * PIECES,))] * 4, dma((10,)), dma((10,)),
            dma, dma, dma,
        ],
        compiler_params=pltpu.CompilerParams(
            collective_id=0, has_side_effects=True, vmem_limit_bytes=60 * 2**20
        ),
        cost_estimate=pl.CostEstimate(
            flops=4 * QALL * BLOCKS * BLK * HD // 2, bytes_accessed=2**21, transcendentals=QALL * 4096
        ),
    )(order, queries.reshape(PART // ROWS, ROWS, 8 * WIDE), keys, values)
    return out.reshape(PART, 8 * WIDE)


def solution(mesh):
    rows = P(("ctx", "head"), None)
    return jax.shard_map(
        shards, mesh=mesh, in_specs=(rows, rows, rows, P()), out_specs=rows, check_vma=False
    )
```

```python
import jax
import jax.numpy as jnp
from jax import lax
from jax.experimental import pallas as pl
from jax.experimental.pallas import tpu as pltpu
from jax.sharding import PartitionSpec as P

MESH = pl.DeviceIdType.MESH
HD = 128
GROUP = 7
PLANES = 8
BLOCKS = 32
PART = 32
ROWS = 8
BLK = 256
QROWS = GROUP * ROWS
QALL = BLOCKS * QROWS
CHUNK = BLOCKS * PART
WIDE = GROUP * HD
TILE = 256
TILES = QALL // TILE
VROWS = HD + 16
SCALE = HD**-0.5 * 1.4426950408889634
MASKED = -1e30

SPAN = [
    ((TILE * t) // QROWS * PART, ((TILE * t + TILE - 1) // QROWS + 1) * PART) for t in range(TILES)
]
EDGE = max(last - first for first, last in SPAN)

PIECES = 4
PIECE = CHUNK // PIECES
TURNS = 3
HALF = CHUNK // 2


def steps(*parts):
    met = [
        (t, tuple((chunk, begin, min(end, last)) for chunk, begin, end in parts if last > begin))
        for t, (first, last) in enumerate(SPAN)
    ]
    met = [step for step in met if step[1]]
    return met[0::2] + met[1::2][::-1]


def low(*chunks):
    return steps(*[(chunk, 0, HALF) for chunk in chunks])


def high(*chunks):
    return steps(*[(chunk, HALF, CHUNK) for chunk in chunks])


def kernel(
    order, q_in, k_in, v_in, out,
    q_held, kv_in, kv_held, q_buf, raw, kv, qs, ones, acc, top, bias, result, o_buf, block_at,
    fetch, q_send, q_recv, q_own, kv_send, kv_recv, kv_own,
    up_send, up_recv, down_send, down_recv, near_send, near_recv, over_send, over_recv,
    o_send, o_recv, o_own,
):
    ctx = lax.axis_index("ctx")
    head = lax.axis_index("head")
    z = lax.rem(head, PLANES)
    y_lo = head // PLANES
    core = lax.rem(ctx, 2)
    g = ctx // 2
    part = 2 * y_lo + core
    me = 2 * ctx + y_lo
    sibling = (ctx + 1 - 2 * core, head)
    above = (ctx, y_lo * PLANES + lax.rem(z + 1, PLANES))
    below = (ctx, y_lo * PLANES + lax.rem(z + PLANES - 1, PLANES))

    def plane_device(index):
        return (index // 2, lax.rem(index, 2) * PLANES + z)

    fetches = [
        pltpu.make_async_copy(k_in, kv_in.at[0], fetch.at[0]),
        pltpu.make_async_copy(v_in, kv_in.at[1], fetch.at[1]),
        pltpu.make_async_copy(q_in, q_held, fetch.at[2]),
    ]
    for copy in fetches:
        copy.start()

    barrier = pltpu.get_barrier_semaphore()

    def greet(i, carry):
        pl.semaphore_signal(
            barrier, inc=1, device_id=plane_device(lax.rem(me + i, 32)), device_id_type=MESH
        )
        return carry

    lax.fori_loop(1, 32, greet, 0)
    for device in (above, below):
        pl.semaphore_signal(barrier, inc=1, device_id=device, device_id_type=MESH)

    fetches[0].wait()
    fetches[1].wait()
    for which in range(2):
        for to_g in range(8):
            kv_held[which, to_g] = kv_in[which, :, to_g * HD : (to_g + 1) * HD]
    own_kv = pltpu.make_async_copy(kv_held.at[core, g], raw.at[me], kv_own)
    own_kv.start()

    pl.semaphore_wait(barrier, 33)

    def send_kv(i, carry):
        target = lax.rem(me + i, 32)
        to_ctx, to_y = target // 2, lax.rem(target, 2)
        pltpu.make_async_remote_copy(
            src_ref=kv_held.at[lax.rem(to_ctx, 2), to_ctx // 2], dst_ref=raw.at[me],
            send_sem=kv_send, recv_sem=kv_recv,
            device_id=(to_ctx, to_y * PLANES + z), device_id_type=MESH,
        ).start()
        return carry

    lax.fori_loop(1, 32, send_kv, 0)

    fetches[2].wait()
    own_q = pltpu.make_async_copy(
        q_held.at[part, :, pl.ds(pl.multiple_of(g * WIDE, HD), WIDE)], q_buf.at[me], q_own
    )
    own_q.start()

    def send_q(i, carry):
        target = lax.rem(me + i, 32)
        to_ctx, to_y = target // 2, lax.rem(target, 2)
        columns = pl.ds(pl.multiple_of(to_ctx // 2 * WIDE, HD), WIDE)
        pltpu.make_async_remote_copy(
            src_ref=q_held.at[2 * to_y + lax.rem(to_ctx, 2), :, columns],
            dst_ref=q_buf.at[me],
            send_sem=q_send,
            recv_sem=q_recv,
            device_id=(to_ctx, to_y * PLANES + z),
            device_id_type=MESH,
        ).start()
        return carry

    lax.fori_loop(1, 32, send_q, 0)

    def piece_of(upward, turn):
        if turn < 2:
            return turn if upward else 1 - turn
        return 2 + y_lo if upward else 3 - y_lo

    def ring(distance, upward, turn):
        if upward:
            chunk, device, sems = lax.rem(z + PLANES + 1 - distance, PLANES), above, (up_send, up_recv)
        else:
            chunk, device, sems = lax.rem(z + distance - 1, PLANES), below, (down_send, down_recv)
        held = kv.at[chunk, core, pl.ds(piece_of(upward, turn) * PIECE, PIECE)]
        index = (distance - 1) * TURNS + turn
        return pltpu.make_async_remote_copy(
            src_ref=held, dst_ref=held,
            send_sem=sems[0].at[index], recv_sem=sems[1].at[index],
            device_id=device, device_id_type=MESH,
        )

    def across(step, chunk, first, count=1):
        held = kv.at[chunk, core, pl.ds(first * PIECE, count * PIECE)]
        return pltpu.make_async_remote_copy(
            src_ref=held, dst_ref=held,
            send_sem=near_send.at[step], recv_sem=near_recv.at[step],
            device_id=sibling, device_id_type=MESH,
        )

    def pass_on(distance, turn):
        ring(distance, True, turn).wait_recv()
        ring(distance, False, turn).wait_recv()

        @pl.when((distance < 3) | (distance == 3) & (turn != 1))
        def _():
            ring(distance + 1, True, turn).start()
            ring(distance + 1, False, turn).start()

        lower, upper = lax.rem(z + PLANES - distance, PLANES), lax.rem(z + distance, PLANES)
        if turn == 2:

            @pl.when(distance < 4)
            def _():
                for chunk, upward in ((lower, True), (upper, False)):
                    over(distance, chunk, piece_of(upward, 2)).start()

        step = 2 * distance + turn // 2
        if turn == 0:
            step = jnp.where(distance == 3, 10, step)
        across(step, lower, piece_of(True, turn)).start()
        across(step, upper, piece_of(False, turn)).start()

    def over(distance, chunk, first, count=1):
        held = kv.at[chunk, core, pl.ds(first * PIECE, count * PIECE)]
        return pltpu.make_async_remote_copy(
            src_ref=held, dst_ref=held,
            send_sem=over_send.at[distance - 1], recv_sem=over_recv.at[distance - 1],
            device_id=(ctx, (1 - y_lo) * PLANES + z), device_id_type=MESH,
        )

    def take_over(distance):
        over(distance, z, 0, 2).wait_recv()
        step = 2 * distance + 1
        across(step, lax.rem(z + PLANES - distance, PLANES), 3 - y_lo).start()
        across(step, lax.rem(z + distance, PLANES), 2 + y_lo).start()

    def from_sibling(step, count):
        held = kv.at[z, 1 - core, pl.ds(0, count * PIECE)]
        pltpu.make_async_copy(held, held, near_recv.at[step]).wait()

    for p in range(BLOCKS):
        at = jnp.int32(0)
        for b in range(BLOCKS):
            at = at + jnp.where(order[b] == p, b, 0)
        block_at[p] = jnp.minimum(at, BLOCKS - 1)
    for t, (first, last) in enumerate(SPAN):
        shape = (last - first, TILE)
        row = lax.broadcasted_iota(jnp.int32, shape, 0) + first
        column = lax.broadcasted_iota(jnp.int32, shape, 1) + t * TILE
        key_block, query_block = row // PART, column // QROWS
        key_row, query_row = lax.rem(row, PART), lax.rem(column, ROWS)
        mine = z * PART + part * ROWS + query_row
        for kind, (key_at, query_at) in enumerate(
            ((0, 0), (z * PART + key_row, mine), (1, 0))
        ):
            kept = key_block * BLK + key_at <= query_block * BLK + query_at
            bias[kind, t, : last - first, :] = jnp.where(kept, 0.0, MASKED)
    ones[...] = jnp.ones_like(ones)
    acc[...] = jnp.zeros_like(acc)
    top[...] = jnp.full_like(top, MASKED)

    own_kv.wait()
    many = raw.at[pl.ds(0, 31)]
    pltpu.make_async_copy(many, many, kv_recv).wait()
    def sort_piece(piece):
        for p in range(piece * 8, piece * 8 + 8, 4):
            rows = jnp.concatenate([raw[block_at[p + i]] for i in range(4)], axis=0)

            @pl.when(core == 0)
            def _():
                kv[z, 0, p * PART : (p + 4) * PART, :] = rows

            @pl.when(core == 1)
            def _():
                kv[z, 1, p * PART : (p + 4) * PART, :] = rows.T

        across(piece // 2, z, piece).start()

    sort_piece(0)
    ring(1, True, 0).start()
    sort_piece(1)
    ring(1, False, 0).start()
    ring(1, True, 1).start()
    ring(1, False, 1).start()
    sort_piece(2)
    sort_piece(3)
    ring(1, True, 2).start()
    ring(1, False, 2).start()

    pass_on(1, 0)
    from_sibling(0, 2)
    own_q.wait()
    many_q = q_buf.at[pl.ds(0, 31)]
    pltpu.make_async_copy(many_q, many_q, q_recv).wait()

    def heads_as_rows(block):
        return jnp.concatenate([block[:, j * HD : (j + 1) * HD] for j in range(GROUP)], axis=0)

    for p in range(0, BLOCKS, 2):
        pair = [heads_as_rows(q_buf[block_at[p + i]]) for i in range(2)]
        qs[p * QROWS : (p + 2) * QROWS, :] = jnp.concatenate(pair, axis=0)

    def attend(steps, between={}):
        def scores(step):
            t, parts = step
            held = [kv[chunk, 0, begin:end, :] for chunk, begin, end in parts]
            held = jnp.concatenate(held, axis=0) if len(held) > 1 else held[0]
            return lax.dot_general(
                held, qs[t * TILE : (t + 1) * TILE, :],
                (((1,), (1,)), ((), ())), preferred_element_type=jnp.float32,
            )

        def weights(step, score):
            t, parts = step
            biased, at = [], 0
            for chunk, begin, end in parts:
                kind = jnp.where(chunk < z, 0, jnp.where(chunk == z, 1, 2))
                edge = min(max(SPAN[t][0], begin), end)
                part = score[at : at + end - begin]
                at += end - begin
                if edge > begin:
                    biased.append(part[: edge - begin])
                if edge < end:
                    rows = slice(edge - SPAN[t][0], end - SPAN[t][0])
                    biased.append(part[edge - begin :] + bias[kind, t, rows, :])
            score = jnp.concatenate(biased, axis=0) if len(biased) > 1 else biased[0]
            old = top[t]
            here = jnp.max(score.reshape(score.shape[0] // 8, 8, TILE), axis=0)
            here = jnp.max(here, axis=0, keepdims=True)
            new = jnp.maximum(old, jnp.broadcast_to(here, (8, TILE)))
            top[t] = new
            weight = jnp.exp2((score - new[0:1]) * SCALE).astype(jnp.bfloat16)
            return weight, jnp.exp2((old - new) * SCALE)

        def add(step, weight, factor):
            t, parts = step
            values = [
                kv[chunk, 1, at : at + HD, : min(HD, end - at)]
                for chunk, begin, end in parts for at in range(begin, end, HD)
            ]
            columns = jnp.concatenate(values, axis=1) if len(values) > 1 else values[0]
            columns = jnp.concatenate([columns, ones[:, : weight.shape[0]]], axis=0)
            acc[t] = acc[t] * factor[0:1] + jnp.dot(columns, weight, preferred_element_type=jnp.float32)

        score, before = scores(steps[0]), None
        for i, step in enumerate(steps):
            following = scores(steps[i + 1]) if i + 1 < len(steps) else None
            current = (step,) + weights(step, score)
            if before is not None:
                add(*before)
            before, score = current, following
            if i in between:
                between[i]()
        add(*before)

    def one_distance(distance, carry):
        lower, upper = lax.rem(z + PLANES - distance, PLANES), lax.rem(z + distance, PLANES)
        alone = (distance == 0) | (distance == 4)

        @pl.when(alone)
        def _():
            def late_first():
                pl.when(distance == 0)(lambda: pass_on(1, 1))

            def take_third():
                pl.when(distance == 4)(lambda: take_over(3))

            def last_first():
                pl.when(distance == 0)(lambda: pass_on(1, 2))

            def late_high():
                @pl.when(distance == 0)
                def _():
                    from_sibling(1, 2)

                @pl.when(distance == 4)
                def _():
                    pass_on(4, 2)
                    from_sibling(9, 2)

            attend(low(upper) + high(upper), {1: late_first, TILES - 3: late_high, TILES: last_first, TILES - 1: take_third})

        @pl.when((distance == 1) | (distance == 2))
        def _():
            def amid():
                pl.when(distance == 1)(lambda: pass_on(2, 0))
                pl.when(distance == 2)(lambda: pass_on(2, 2))

            def late():
                pl.when(distance == 2)(lambda: take_over(1))

            def last():
                pl.when(distance == 1)(lambda: pass_on(2, 1))
                pl.when(distance == 2)(lambda: pass_on(3, 0))

            from_sibling(2 * distance, 4)
            attend(low(lower, upper), {0: amid, 2: late, 3: last})

        @pl.when(distance == 3)
        def _():
            from_sibling(10, 2)
            so_far = steps((lower, 0, PIECE), (upper, PIECE, HALF))
            rest = steps((lower, PIECE, HALF), (upper, 0, PIECE))
            attend(
                so_far + rest,
                {
                    0: lambda: pass_on(3, 1),
                    TILES - 2: lambda: from_sibling(6, 2),
                    TILES - 1: lambda: pass_on(3, 2),
                    TILES + 1: lambda: take_over(2),
                    TILES + 2: lambda: pass_on(4, 0),
                },
            )

        @pl.when(distance > 1)
        def _():
            from_sibling(2 * distance - 1, 4)
            attend(high(lax.rem(lower + 1, PLANES), lax.rem(upper + PLANES - 1, PLANES)))
            pl.when(distance == 3)(lambda: from_sibling(8, 2))

        return carry

    lax.fori_loop(0, 5, one_distance, 0)

    for t in range(TILES):
        total = acc[t]
        rows = (total[:HD] * (1.0 / total[HD : HD + 1])).T
        at = t * TILE
        while at < (t + 1) * TILE:
            block, row = at // QROWS, at % QROWS
            count = min(QROWS - row, (t + 1) * TILE - at)
            result[block, row : row + count, :] = rows[at - t * TILE : at - t * TILE + count]
            at += count

    def out_copy(b, device_rows):
        return out.at[device_rows, :, pl.ds(pl.multiple_of(g * WIDE, HD), WIDE)]

    def send_back(group, carry):
        indices = [4 * group + 1 + j for j in range(4)]
        blocks = [lax.rem(me + i, BLOCKS) for i in indices]
        for b in blocks:
            rows = result[order[b]].astype(jnp.bfloat16)
            o_buf[b] = jnp.concatenate([rows[j * ROWS : (j + 1) * ROWS] for j in range(GROUP)], axis=1)
        for i, b in zip(indices, blocks):

            @pl.when(i < BLOCKS)
            def _():
                pltpu.make_async_remote_copy(
                    src_ref=o_buf.at[b], dst_ref=out_copy(b, part),
                    send_sem=o_send, recv_sem=o_recv,
                    device_id=plane_device(b), device_id_type=MESH,
                ).start()

        return carry

    lax.fori_loop(0, BLOCKS // 4, send_back, 0)
    own_o = pltpu.make_async_copy(o_buf.at[me], out_copy(me, part), o_own)
    own_o.start()

    many_o = o_buf.at[pl.ds(0, 31)]
    pltpu.make_async_copy(many_q, many_q, q_send).wait()
    pltpu.make_async_copy(many, many, kv_send).wait()
    for distance in range(1, 5):
        for turn in range(0, TURNS, 1 if distance < 4 else 2):
            ring(distance, True, turn).wait_send()
            ring(distance, False, turn).wait_send()
        if distance < 4:
            over(distance, z, 0, 2).wait_send()
    for step in range(11):
        across(step, z, 0, 4 if step in (2, 3, 4, 5, 7) else 2).wait_send()
    own_o.wait()
    pltpu.make_async_copy(many_o, many_o, o_send).wait()
    pltpu.make_async_copy(many_o, many_o, o_recv).wait()


def shards(queries, keys, values, order):
    hbm = pl.BlockSpec(memory_space=pltpu.HBM)
    dma = pltpu.SemaphoreType.DMA
    out = pl.pallas_call(
        kernel,
        out_shape=pltpu.VMEM((PART // ROWS, ROWS, 8 * WIDE), jnp.bfloat16),
        in_specs=[pl.BlockSpec(memory_space=pltpu.SMEM), hbm, hbm, hbm],
        out_specs=pl.BlockSpec(memory_space=pltpu.VMEM),
        scratch_shapes=[
            pltpu.VMEM((PART // ROWS, ROWS, 8 * WIDE), jnp.bfloat16),
            pltpu.VMEM((2, PART, 8 * HD), jnp.bfloat16),
            pltpu.VMEM((2, 8, PART, HD), jnp.bfloat16),
            pltpu.VMEM((BLOCKS, ROWS, WIDE), jnp.bfloat16),
            pltpu.VMEM((BLOCKS, PART, HD), jnp.bfloat16),
            pltpu.VMEM((PLANES, 2, CHUNK, HD), jnp.bfloat16),
            pltpu.VMEM((QALL, HD), jnp.bfloat16),
            pltpu.VMEM((VROWS - HD, CHUNK), jnp.bfloat16),
            pltpu.VMEM((TILES, VROWS, TILE), jnp.float32),
            pltpu.VMEM((TILES, 8, TILE), jnp.float32),
            pltpu.VMEM((3, TILES, EDGE, TILE), jnp.float32),
            pltpu.VMEM((BLOCKS, QROWS, HD), jnp.float32),
            pltpu.VMEM((BLOCKS, ROWS, WIDE), jnp.bfloat16),
            pltpu.SMEM((BLOCKS,), jnp.int32),
            dma((3,)), dma, dma, dma, dma, dma, dma,
            *[dma((4 * TURNS,))] * 4, dma((11,)), dma((11,)), dma((3,)), dma((3,)),
            dma, dma, dma,
        ],
        compiler_params=pltpu.CompilerParams(
            collective_id=0, has_side_effects=True, vmem_limit_bytes=60 * 2**20
        ),
        cost_estimate=pl.CostEstimate(
            flops=4 * QALL * BLOCKS * BLK * HD // 2, bytes_accessed=2**21, transcendentals=QALL * 4096
        ),
    )(order, queries.reshape(PART // ROWS, ROWS, 8 * WIDE), keys, values)
    return out.reshape(PART, 8 * WIDE)


def solution(mesh):
    rows = P(("ctx", "head"), None)
    return jax.shard_map(
        shards, mesh=mesh, in_specs=(rows, rows, rows, P()), out_specs=rows, check_vma=False
    )
```

```python
import jax
import jax.numpy as jnp
from jax import lax
from jax.experimental import pallas as pl
from jax.experimental.pallas import tpu as pltpu
from jax.sharding import PartitionSpec as P

MESH = pl.DeviceIdType.MESH
HD = 128
GROUP = 7
PLANES = 8
BLOCKS = 32
PART = 32
ROWS = 8
BLK = 256
QROWS = GROUP * ROWS
QALL = BLOCKS * QROWS
CHUNK = BLOCKS * PART
WIDE = GROUP * HD
TILE = 256
TILES = QALL // TILE
VROWS = HD + 16
SCALE = HD**-0.5 * 1.4426950408889634
MASKED = -1e30

SPAN = [
    ((TILE * t) // QROWS * PART, ((TILE * t + TILE - 1) // QROWS + 1) * PART) for t in range(TILES)
]
EDGE = max(last - first for first, last in SPAN)

PIECES = 4
PIECE = CHUNK // PIECES
TURNS = 3
HALF = CHUNK // 2


def steps(*parts):
    met = [
        (t, tuple((chunk, begin, min(end, last)) for chunk, begin, end in parts if last > begin))
        for t, (first, last) in enumerate(SPAN)
    ]
    met = [step for step in met if step[1]]
    return met[0::2] + met[1::2][::-1]


def low(*chunks):
    return steps(*[(chunk, 0, HALF) for chunk in chunks])


def high(*chunks):
    return steps(*[(chunk, HALF, CHUNK) for chunk in chunks])


def kernel(
    order, q_in, k_in, v_in, out,
    q_held, kv_in, kv_held, q_buf, raw, kv, qs, ones, acc, top, bias, result, o_buf, block_at,
    fetch, q_send, q_recv, q_own, kv_send, kv_recv, kv_own,
    up_send, up_recv, down_send, down_recv, near_send, near_recv, over_send, over_recv,
    o_send, o_recv, o_own,
):
    ctx = lax.axis_index("ctx")
    head = lax.axis_index("head")
    z = lax.rem(head, PLANES)
    y_lo = head // PLANES
    core = lax.rem(ctx, 2)
    g = ctx // 2
    part = 2 * y_lo + core
    me = 2 * ctx + y_lo
    sibling = (ctx + 1 - 2 * core, head)
    above = (ctx, y_lo * PLANES + lax.rem(z + 1, PLANES))
    below = (ctx, y_lo * PLANES + lax.rem(z + PLANES - 1, PLANES))

    def plane_device(index):
        return (index // 2, lax.rem(index, 2) * PLANES + z)

    fetches = [
        pltpu.make_async_copy(k_in, kv_in.at[0], fetch.at[0]),
        pltpu.make_async_copy(v_in, kv_in.at[1], fetch.at[1]),
        pltpu.make_async_copy(q_in, q_held, fetch.at[2]),
    ]
    for copy in fetches:
        copy.start()

    barrier = pltpu.get_barrier_semaphore()

    def greet(i, carry):
        pl.semaphore_signal(
            barrier, inc=1, device_id=plane_device(lax.rem(me + i, 32)), device_id_type=MESH
        )
        return carry

    lax.fori_loop(1, 32, greet, 0)
    for device in (above, below):
        pl.semaphore_signal(barrier, inc=1, device_id=device, device_id_type=MESH)

    fetches[0].wait()
    fetches[1].wait()
    for which in range(2):
        for to_g in range(8):
            kv_held[which, to_g] = kv_in[which, :, to_g * HD : (to_g + 1) * HD]
    own_kv = pltpu.make_async_copy(kv_held.at[core, g], raw.at[me], kv_own)
    own_kv.start()

    pl.semaphore_wait(barrier, 33)

    def send_kv(i, carry):
        target = lax.rem(me + i, 32)
        to_ctx, to_y = target // 2, lax.rem(target, 2)
        pltpu.make_async_remote_copy(
            src_ref=kv_held.at[lax.rem(to_ctx, 2), to_ctx // 2], dst_ref=raw.at[me],
            send_sem=kv_send, recv_sem=kv_recv,
            device_id=(to_ctx, to_y * PLANES + z), device_id_type=MESH,
        ).start()
        return carry

    lax.fori_loop(1, 32, send_kv, 0)

    fetches[2].wait()
    own_q = pltpu.make_async_copy(
        q_held.at[part, :, pl.ds(pl.multiple_of(g * WIDE, HD), WIDE)], q_buf.at[me], q_own
    )
    own_q.start()

    def send_q(i, carry):
        target = lax.rem(me + i, 32)
        to_ctx, to_y = target // 2, lax.rem(target, 2)
        columns = pl.ds(pl.multiple_of(to_ctx // 2 * WIDE, HD), WIDE)
        pltpu.make_async_remote_copy(
            src_ref=q_held.at[2 * to_y + lax.rem(to_ctx, 2), :, columns],
            dst_ref=q_buf.at[me],
            send_sem=q_send,
            recv_sem=q_recv,
            device_id=(to_ctx, to_y * PLANES + z),
            device_id_type=MESH,
        ).start()
        return carry

    lax.fori_loop(1, 32, send_q, 0)

    def piece_of(upward, turn):
        if turn < 2:
            return turn if upward else 1 - turn
        return 2 + y_lo if upward else 3 - y_lo

    def ring(distance, upward, turn):
        if upward:
            chunk, device, sems = lax.rem(z + PLANES + 1 - distance, PLANES), above, (up_send, up_recv)
        else:
            chunk, device, sems = lax.rem(z + distance - 1, PLANES), below, (down_send, down_recv)
        held = kv.at[chunk, core, pl.ds(piece_of(upward, turn) * PIECE, PIECE)]
        index = (distance - 1) * TURNS + turn
        return pltpu.make_async_remote_copy(
            src_ref=held, dst_ref=held,
            send_sem=sems[0].at[index], recv_sem=sems[1].at[index],
            device_id=device, device_id_type=MESH,
        )

    def across(step, chunk, first, count=1):
        held = kv.at[chunk, core, pl.ds(first * PIECE, count * PIECE)]
        return pltpu.make_async_remote_copy(
            src_ref=held, dst_ref=held,
            send_sem=near_send.at[step], recv_sem=near_recv.at[step],
            device_id=sibling, device_id_type=MESH,
        )

    def pass_on(distance, turn):
        step = 2 * distance + turn // 2
        if turn == 0:
            step = jnp.where(distance == 3, 10, step)
        for upward in (True, False):
            chunk = lax.rem(z + (PLANES - distance if upward else distance), PLANES)
            ring(distance, upward, turn).wait_recv()
            if turn == 2:
                pl.when(distance < 4)(lambda: over(distance, chunk, piece_of(upward, 2)).start())
            pl.when((distance < 3) | (distance == 3) & (turn != 1))(
                lambda: ring(distance + 1, upward, turn).start()
            )
            across(step, chunk, piece_of(upward, turn)).start()

    def over(distance, chunk, first, count=1):
        held = kv.at[chunk, core, pl.ds(first * PIECE, count * PIECE)]
        return pltpu.make_async_remote_copy(
            src_ref=held, dst_ref=held,
            send_sem=over_send.at[distance - 1], recv_sem=over_recv.at[distance - 1],
            device_id=(ctx, (1 - y_lo) * PLANES + z), device_id_type=MESH,
        )

    def take_over(distance):
        over(distance, z, 0, 2).wait_recv()
        step = 2 * distance + 1
        across(step, lax.rem(z + PLANES - distance, PLANES), 3 - y_lo).start()
        across(step, lax.rem(z + distance, PLANES), 2 + y_lo).start()

    def from_sibling(step, count):
        held = kv.at[z, 1 - core, pl.ds(0, count * PIECE)]
        pltpu.make_async_copy(held, held, near_recv.at[step]).wait()

    for p in range(BLOCKS):
        at = jnp.int32(0)
        for b in range(BLOCKS):
            at = at + jnp.where(order[b] == p, b, 0)
        block_at[p] = jnp.minimum(at, BLOCKS - 1)
    for t, (first, last) in enumerate(SPAN):
        shape = (last - first, TILE)
        row = lax.broadcasted_iota(jnp.int32, shape, 0) + first
        column = lax.broadcasted_iota(jnp.int32, shape, 1) + t * TILE
        key_block, query_block = row // PART, column // QROWS
        key_row, query_row = lax.rem(row, PART), lax.rem(column, ROWS)
        mine = z * PART + part * ROWS + query_row
        for kind, (key_at, query_at) in enumerate(
            ((0, 0), (z * PART + key_row, mine), (1, 0))
        ):
            kept = key_block * BLK + key_at <= query_block * BLK + query_at
            bias[kind, t, : last - first, :] = jnp.where(kept, 0.0, MASKED)
    ones[...] = jnp.ones_like(ones)
    acc[...] = jnp.zeros_like(acc)
    top[...] = jnp.full_like(top, MASKED)

    own_kv.wait()
    many = raw.at[pl.ds(0, 31)]
    pltpu.make_async_copy(many, many, kv_recv).wait()
    def sort_piece(piece):
        for p in range(piece * 8, piece * 8 + 8, 4):
            rows = jnp.concatenate([raw[block_at[p + i]] for i in range(4)], axis=0)

            @pl.when(core == 0)
            def _():
                kv[z, 0, p * PART : (p + 4) * PART, :] = rows

            @pl.when(core == 1)
            def _():
                kv[z, 1, p * PART : (p + 4) * PART, :] = rows.T

        across(piece // 2, z, piece).start()

    sort_piece(0)
    ring(1, True, 0).start()
    sort_piece(1)
    ring(1, False, 0).start()
    ring(1, True, 1).start()
    ring(1, False, 1).start()
    sort_piece(2)
    sort_piece(3)
    ring(1, True, 2).start()
    ring(1, False, 2).start()

    pass_on(1, 0)
    from_sibling(0, 2)
    own_q.wait()
    many_q = q_buf.at[pl.ds(0, 31)]
    pltpu.make_async_copy(many_q, many_q, q_recv).wait()

    def heads_as_rows(block):
        return jnp.concatenate([block[:, j * HD : (j + 1) * HD] for j in range(GROUP)], axis=0)

    for p in range(0, BLOCKS, 2):
        pair = [heads_as_rows(q_buf[block_at[p + i]]) for i in range(2)]
        qs[p * QROWS : (p + 2) * QROWS, :] = jnp.concatenate(pair, axis=0)

    def attend(steps, between={}):
        def scores(step):
            t, parts = step
            held = [kv[chunk, 0, begin:end, :] for chunk, begin, end in parts]
            held = jnp.concatenate(held, axis=0) if len(held) > 1 else held[0]
            return lax.dot_general(
                held, qs[t * TILE : (t + 1) * TILE, :],
                (((1,), (1,)), ((), ())), preferred_element_type=jnp.float32,
            )

        def weights(step, score):
            t, parts = step
            biased, at = [], 0
            for chunk, begin, end in parts:
                kind = jnp.where(chunk < z, 0, jnp.where(chunk == z, 1, 2))
                edge = min(max(SPAN[t][0], begin), end)
                part = score[at : at + end - begin]
                at += end - begin
                if edge > begin:
                    biased.append(part[: edge - begin])
                if edge < end:
                    rows = slice(edge - SPAN[t][0], end - SPAN[t][0])
                    biased.append(part[edge - begin :] + bias[kind, t, rows, :])
            score = jnp.concatenate(biased, axis=0) if len(biased) > 1 else biased[0]
            old = top[t]
            here = jnp.max(score.reshape(score.shape[0] // 8, 8, TILE), axis=0)
            here = jnp.max(here, axis=0, keepdims=True)
            new = jnp.maximum(old, jnp.broadcast_to(here, (8, TILE)))
            top[t] = new
            weight = jnp.exp2((score - new[0:1]) * SCALE).astype(jnp.bfloat16)
            return weight, jnp.exp2((old - new) * SCALE)

        def add(step, weight, factor):
            t, parts = step
            values = [
                kv[chunk, 1, at : at + HD, : min(HD, end - at)]
                for chunk, begin, end in parts for at in range(begin, end, HD)
            ]
            columns = jnp.concatenate(values, axis=1) if len(values) > 1 else values[0]
            columns = jnp.concatenate([columns, ones[:, : weight.shape[0]]], axis=0)
            acc[t] = acc[t] * factor[0:1] + jnp.dot(columns, weight, preferred_element_type=jnp.float32)

        score, before = scores(steps[0]), None
        for i, step in enumerate(steps):
            following = scores(steps[i + 1]) if i + 1 < len(steps) else None
            current = (step,) + weights(step, score)
            if before is not None:
                add(*before)
            before, score = current, following
            if i in between:
                between[i]()
        add(*before)

    def one_distance(distance, carry):
        lower, upper = lax.rem(z + PLANES - distance, PLANES), lax.rem(z + distance, PLANES)
        alone = (distance == 0) | (distance == 4)

        @pl.when(alone)
        def _():
            def late_first():
                pl.when(distance == 0)(lambda: pass_on(1, 1))

            def take_third():
                pl.when(distance == 4)(lambda: take_over(3))

            def last_first():
                pl.when(distance == 0)(lambda: pass_on(1, 2))

            def late_high():
                @pl.when(distance == 0)
                def _():
                    from_sibling(1, 2)

                @pl.when(distance == 4)
                def _():
                    pass_on(4, 2)
                    from_sibling(9, 2)

            attend(low(upper) + high(upper), {1: late_first, TILES - 3: late_high, TILES: last_first, TILES - 1: take_third})

        @pl.when((distance == 1) | (distance == 2))
        def _():
            def amid():
                pl.when(distance == 1)(lambda: pass_on(2, 0))
                pl.when(distance == 2)(lambda: pass_on(2, 2))

            def late():
                pl.when(distance == 2)(lambda: take_over(1))

            def last():
                pl.when(distance == 1)(lambda: pass_on(2, 1))
                pl.when(distance == 2)(lambda: pass_on(3, 0))

            from_sibling(2 * distance, 4)
            attend(low(lower, upper), {0: amid, 2: late, 3: last})

        @pl.when(distance == 3)
        def _():
            from_sibling(10, 2)
            so_far = steps((lower, 0, PIECE), (upper, PIECE, HALF))
            rest = steps((lower, PIECE, HALF), (upper, 0, PIECE))
            attend(
                so_far + rest,
                {
                    0: lambda: pass_on(3, 1),
                    TILES - 2: lambda: from_sibling(6, 2),
                    TILES - 1: lambda: pass_on(3, 2),
                    TILES + 1: lambda: take_over(2),
                    TILES + 2: lambda: pass_on(4, 0),
                },
            )

        @pl.when(distance > 1)
        def _():
            from_sibling(2 * distance - 1, 4)
            attend(high(lax.rem(lower + 1, PLANES), lax.rem(upper + PLANES - 1, PLANES)))
            pl.when(distance == 3)(lambda: from_sibling(8, 2))

        return carry

    lax.fori_loop(0, 5, one_distance, 0)

    for t in range(TILES):
        total = acc[t]
        rows = (total[:HD] * (1.0 / total[HD : HD + 1])).T
        at = t * TILE
        while at < (t + 1) * TILE:
            block, row = at // QROWS, at % QROWS
            count = min(QROWS - row, (t + 1) * TILE - at)
            result[block, row : row + count, :] = rows[at - t * TILE : at - t * TILE + count]
            at += count

    def out_copy(b, device_rows):
        return out.at[device_rows, :, pl.ds(pl.multiple_of(g * WIDE, HD), WIDE)]

    def send_back(group, carry):
        indices = [4 * group + 1 + j for j in range(4)]
        blocks = [lax.rem(me + i, BLOCKS) for i in indices]
        for b in blocks:
            rows = result[order[b]].astype(jnp.bfloat16)
            o_buf[b] = jnp.concatenate([rows[j * ROWS : (j + 1) * ROWS] for j in range(GROUP)], axis=1)
        for i, b in zip(indices, blocks):

            @pl.when(i < BLOCKS)
            def _():
                pltpu.make_async_remote_copy(
                    src_ref=o_buf.at[b], dst_ref=out_copy(b, part),
                    send_sem=o_send, recv_sem=o_recv,
                    device_id=plane_device(b), device_id_type=MESH,
                ).start()

        return carry

    lax.fori_loop(0, BLOCKS // 4, send_back, 0)
    own_o = pltpu.make_async_copy(o_buf.at[me], out_copy(me, part), o_own)
    own_o.start()

    many_o = o_buf.at[pl.ds(0, 31)]
    pltpu.make_async_copy(many_q, many_q, q_send).wait()
    pltpu.make_async_copy(many, many, kv_send).wait()
    for distance in range(1, 5):
        for turn in range(0, TURNS, 1 if distance < 4 else 2):
            ring(distance, True, turn).wait_send()
            ring(distance, False, turn).wait_send()
        if distance < 4:
            over(distance, z, 0, 2).wait_send()
    for step in range(11):
        across(step, z, 0, 4 if step in (2, 3, 4, 5, 7) else 2).wait_send()
    own_o.wait()
    pltpu.make_async_copy(many_o, many_o, o_send).wait()
    pltpu.make_async_copy(many_o, many_o, o_recv).wait()


def shards(queries, keys, values, order):
    hbm = pl.BlockSpec(memory_space=pltpu.HBM)
    dma = pltpu.SemaphoreType.DMA
    out = pl.pallas_call(
        kernel,
        out_shape=pltpu.VMEM((PART // ROWS, ROWS, 8 * WIDE), jnp.bfloat16),
        in_specs=[pl.BlockSpec(memory_space=pltpu.SMEM), hbm, hbm, hbm],
        out_specs=pl.BlockSpec(memory_space=pltpu.VMEM),
        scratch_shapes=[
            pltpu.VMEM((PART // ROWS, ROWS, 8 * WIDE), jnp.bfloat16),
            pltpu.VMEM((2, PART, 8 * HD), jnp.bfloat16),
            pltpu.VMEM((2, 8, PART, HD), jnp.bfloat16),
            pltpu.VMEM((BLOCKS, ROWS, WIDE), jnp.bfloat16),
            pltpu.VMEM((BLOCKS, PART, HD), jnp.bfloat16),
            pltpu.VMEM((PLANES, 2, CHUNK, HD), jnp.bfloat16),
            pltpu.VMEM((QALL, HD), jnp.bfloat16),
            pltpu.VMEM((VROWS - HD, CHUNK), jnp.bfloat16),
            pltpu.VMEM((TILES, VROWS, TILE), jnp.float32),
            pltpu.VMEM((TILES, 8, TILE), jnp.float32),
            pltpu.VMEM((3, TILES, EDGE, TILE), jnp.float32),
            pltpu.VMEM((BLOCKS, QROWS, HD), jnp.float32),
            pltpu.VMEM((BLOCKS, ROWS, WIDE), jnp.bfloat16),
            pltpu.SMEM((BLOCKS,), jnp.int32),
            dma((3,)), dma, dma, dma, dma, dma, dma,
            *[dma((4 * TURNS,))] * 4, dma((11,)), dma((11,)), dma((3,)), dma((3,)),
            dma, dma, dma,
        ],
        compiler_params=pltpu.CompilerParams(
            collective_id=0, has_side_effects=True, vmem_limit_bytes=60 * 2**20
        ),
        cost_estimate=pl.CostEstimate(
            flops=4 * QALL * BLOCKS * BLK * HD // 2, bytes_accessed=2**21, transcendentals=QALL * 4096
        ),
    )(order, queries.reshape(PART // ROWS, ROWS, 8 * WIDE), keys, values)
    return out.reshape(PART, 8 * WIDE)


def solution(mesh):
    rows = P(("ctx", "head"), None)
    return jax.shard_map(
        shards, mesh=mesh, in_specs=(rows, rows, rows, P()), out_specs=rows, check_vma=False
    )
```

```python
import jax
import jax.numpy as jnp
from jax import lax
from jax.experimental import pallas as pl
from jax.experimental.pallas import tpu as pltpu
from jax.sharding import PartitionSpec as P

MESH = pl.DeviceIdType.MESH
HD = 128
GROUP = 7
PLANES = 8
BLOCKS = 32
PART = 32
ROWS = 8
BLK = 256
QROWS = GROUP * ROWS
QALL = BLOCKS * QROWS
CHUNK = BLOCKS * PART
WIDE = GROUP * HD
TILE = 256
TILES = QALL // TILE
VROWS = HD + 16
SCALE = HD**-0.5 * 1.4426950408889634
MASKED = -1e30

SPAN = [
    ((TILE * t) // QROWS * PART, ((TILE * t + TILE - 1) // QROWS + 1) * PART) for t in range(TILES)
]
EDGE = max(last - first for first, last in SPAN)

PIECES = 4
PIECE = CHUNK // PIECES
TURNS = 3
HALF = CHUNK // 2


def steps(*parts):
    met = [
        (t, tuple((chunk, begin, min(end, last)) for chunk, begin, end in parts if last > begin))
        for t, (first, last) in enumerate(SPAN)
    ]
    met = [step for step in met if step[1]]
    return met[0::2] + met[1::2][::-1]


def low(*chunks):
    return steps(*[(chunk, 0, HALF) for chunk in chunks])


def high(*chunks):
    return steps(*[(chunk, HALF, CHUNK) for chunk in chunks])


def kernel(
    order, q_in, k_in, v_in, out,
    q_held, kv_in, kv_held, q_buf, raw, kv, qs, ones, acc, top, bias, result, o_buf, block_at,
    fetch, q_send, q_recv, q_own, kv_send, kv_recv, kv_own,
    up_send, up_recv, down_send, down_recv, near_send, near_recv, over_send, over_recv,
    o_send, o_recv, o_own,
):
    ctx = lax.axis_index("ctx")
    head = lax.axis_index("head")
    z = lax.rem(head, PLANES)
    y_lo = head // PLANES
    core = lax.rem(ctx, 2)
    g = ctx // 2
    part = 2 * y_lo + core
    me = 2 * ctx + y_lo
    sibling = (ctx + 1 - 2 * core, head)
    above = (ctx, y_lo * PLANES + lax.rem(z + 1, PLANES))
    below = (ctx, y_lo * PLANES + lax.rem(z + PLANES - 1, PLANES))

    def plane_device(index):
        return (index // 2, lax.rem(index, 2) * PLANES + z)

    fetches = [
        pltpu.make_async_copy(k_in, kv_in.at[0], fetch.at[0]),
        pltpu.make_async_copy(v_in, kv_in.at[1], fetch.at[1]),
        pltpu.make_async_copy(q_in, q_held, fetch.at[2]),
    ]
    for copy in fetches:
        copy.start()

    barrier = pltpu.get_barrier_semaphore()

    def greet(i, carry):
        pl.semaphore_signal(
            barrier, inc=1, device_id=plane_device(lax.rem(me + i, 32)), device_id_type=MESH
        )
        return carry

    lax.fori_loop(1, 32, greet, 0)
    for device in (above, below):
        pl.semaphore_signal(barrier, inc=1, device_id=device, device_id_type=MESH)

    fetches[0].wait()
    fetches[1].wait()
    for which in range(2):
        for to_g in range(8):
            kv_held[which, to_g] = kv_in[which, :, to_g * HD : (to_g + 1) * HD]
    own_kv = pltpu.make_async_copy(kv_held.at[core, g], raw.at[me], kv_own)
    own_kv.start()

    pl.semaphore_wait(barrier, 33)

    def send_kv(i, carry):
        target = lax.rem(me + i, 32)
        to_ctx, to_y = target // 2, lax.rem(target, 2)
        pltpu.make_async_remote_copy(
            src_ref=kv_held.at[lax.rem(to_ctx, 2), to_ctx // 2], dst_ref=raw.at[me],
            send_sem=kv_send, recv_sem=kv_recv,
            device_id=(to_ctx, to_y * PLANES + z), device_id_type=MESH,
        ).start()
        return carry

    lax.fori_loop(1, 32, send_kv, 0)

    fetches[2].wait()
    own_q = pltpu.make_async_copy(
        q_held.at[part, :, pl.ds(pl.multiple_of(g * WIDE, HD), WIDE)], q_buf.at[me], q_own
    )
    own_q.start()

    def send_q(i, carry):
        target = lax.rem(me + i, 32)
        to_ctx, to_y = target // 2, lax.rem(target, 2)
        columns = pl.ds(pl.multiple_of(to_ctx // 2 * WIDE, HD), WIDE)
        pltpu.make_async_remote_copy(
            src_ref=q_held.at[2 * to_y + lax.rem(to_ctx, 2), :, columns],
            dst_ref=q_buf.at[me],
            send_sem=q_send,
            recv_sem=q_recv,
            device_id=(to_ctx, to_y * PLANES + z),
            device_id_type=MESH,
        ).start()
        return carry

    lax.fori_loop(1, 32, send_q, 0)

    def piece_of(upward, turn):
        if turn < 2:
            return turn if upward else 1 - turn
        return 2 + y_lo if upward else 3 - y_lo

    def ring(distance, upward, turn):
        if upward:
            chunk, device, sems = lax.rem(z + PLANES + 1 - distance, PLANES), above, (up_send, up_recv)
        else:
            chunk, device, sems = lax.rem(z + distance - 1, PLANES), below, (down_send, down_recv)
        held = kv.at[chunk, core, pl.ds(piece_of(upward, turn) * PIECE, PIECE)]
        index = (distance - 1) * TURNS + turn
        return pltpu.make_async_remote_copy(
            src_ref=held, dst_ref=held,
            send_sem=sems[0].at[index], recv_sem=sems[1].at[index],
            device_id=device, device_id_type=MESH,
        )

    def across(step, chunk, first, count=1):
        held = kv.at[chunk, core, pl.ds(first * PIECE, count * PIECE)]
        return pltpu.make_async_remote_copy(
            src_ref=held, dst_ref=held,
            send_sem=near_send.at[step], recv_sem=near_recv.at[step],
            device_id=sibling, device_id_type=MESH,
        )

    def pass_on(distance, turn):
        step = 2 * distance + turn // 2
        if turn == 0:
            step = jnp.where(distance == 3, 10, step)
        for upward in (True, False):
            chunk = lax.rem(z + (PLANES - distance if upward else distance), PLANES)
            ring(distance, upward, turn).wait_recv()
            if turn == 2:
                pl.when(distance < 4)(lambda: over(distance, chunk, piece_of(upward, 2)).start())
            pl.when((distance < 3) | (distance == 3) & (turn != 1))(
                lambda: ring(distance + 1, upward, turn).start()
            )
            across(step, chunk, piece_of(upward, turn)).start()

    def over(distance, chunk, first, count=1):
        held = kv.at[chunk, core, pl.ds(first * PIECE, count * PIECE)]
        return pltpu.make_async_remote_copy(
            src_ref=held, dst_ref=held,
            send_sem=over_send.at[distance - 1], recv_sem=over_recv.at[distance - 1],
            device_id=(ctx, (1 - y_lo) * PLANES + z), device_id_type=MESH,
        )

    def take_over(distance):
        over(distance, z, 0, 2).wait_recv()
        step = 2 * distance + 1
        across(step, lax.rem(z + PLANES - distance, PLANES), 3 - y_lo).start()
        across(step, lax.rem(z + distance, PLANES), 2 + y_lo).start()

    def from_sibling(step, count):
        held = kv.at[z, 1 - core, pl.ds(0, count * PIECE)]
        pltpu.make_async_copy(held, held, near_recv.at[step]).wait()

    for p in range(BLOCKS):
        at = jnp.int32(0)
        for b in range(BLOCKS):
            at = at + jnp.where(order[b] == p, b, 0)
        block_at[p] = jnp.minimum(at, BLOCKS - 1)
    for t, (first, last) in enumerate(SPAN):
        shape = (last - first, TILE)
        row = lax.broadcasted_iota(jnp.int32, shape, 0) + first
        column = lax.broadcasted_iota(jnp.int32, shape, 1) + t * TILE
        key_block, query_block = row // PART, column // QROWS
        key_row, query_row = lax.rem(row, PART), lax.rem(column, ROWS)
        mine = z * PART + part * ROWS + query_row
        for kind, (key_at, query_at) in enumerate(
            ((0, 0), (z * PART + key_row, mine), (1, 0))
        ):
            kept = key_block * BLK + key_at <= query_block * BLK + query_at
            bias[kind, t, : last - first, :] = jnp.where(kept, 0.0, MASKED)
    ones[...] = jnp.ones_like(ones)
    acc[...] = jnp.zeros_like(acc)
    top[...] = jnp.full_like(top, MASKED)

    own_kv.wait()
    many = raw.at[pl.ds(0, 31)]
    pltpu.make_async_copy(many, many, kv_recv).wait()
    def sort_piece(piece):
        for p in range(piece * 8, piece * 8 + 8, 4):
            rows = jnp.concatenate([raw[block_at[p + i]] for i in range(4)], axis=0)

            @pl.when(core == 0)
            def _():
                kv[z, 0, p * PART : (p + 4) * PART, :] = rows

            @pl.when(core == 1)
            def _():
                kv[z, 1, p * PART : (p + 4) * PART, :] = rows.T

        across(piece // 2, z, piece).start()

    sort_piece(0)
    ring(1, True, 0).start()
    sort_piece(1)
    ring(1, False, 0).start()
    ring(1, True, 1).start()
    ring(1, False, 1).start()
    sort_piece(2)
    sort_piece(3)
    ring(1, True, 2).start()
    ring(1, False, 2).start()

    pass_on(1, 0)
    from_sibling(0, 2)
    own_q.wait()
    many_q = q_buf.at[pl.ds(0, 31)]
    pltpu.make_async_copy(many_q, many_q, q_recv).wait()

    def heads_as_rows(block):
        return jnp.concatenate([block[:, j * HD : (j + 1) * HD] for j in range(GROUP)], axis=0)

    for p in range(0, BLOCKS, 2):
        pair = [heads_as_rows(q_buf[block_at[p + i]]) for i in range(2)]
        qs[p * QROWS : (p + 2) * QROWS, :] = jnp.concatenate(pair, axis=0)

    def attend(steps, between={}):
        def scores(step):
            t, parts = step
            held = [kv[chunk, 0, begin:end, :] for chunk, begin, end in parts]
            held = jnp.concatenate(held, axis=0) if len(held) > 1 else held[0]
            return lax.dot_general(
                held, qs[t * TILE : (t + 1) * TILE, :],
                (((1,), (1,)), ((), ())), preferred_element_type=jnp.float32,
            )

        def weights(step, score):
            t, parts = step
            biased, at = [], 0
            for chunk, begin, end in parts:
                kind = jnp.where(chunk < z, 0, jnp.where(chunk == z, 1, 2))
                edge = min(max(SPAN[t][0], begin), end)
                part = score[at : at + end - begin]
                at += end - begin
                if edge > begin:
                    biased.append(part[: edge - begin])
                if edge < end:
                    rows = slice(edge - SPAN[t][0], end - SPAN[t][0])
                    biased.append(part[edge - begin :] + bias[kind, t, rows, :])
            score = jnp.concatenate(biased, axis=0) if len(biased) > 1 else biased[0]
            old = top[t]
            here = jnp.max(score.reshape(score.shape[0] // 8, 8, TILE), axis=0)
            here = jnp.max(here, axis=0, keepdims=True)
            new = jnp.maximum(old, jnp.broadcast_to(here, (8, TILE)))
            top[t] = new
            weight = jnp.exp2((score - new[0:1]) * SCALE).astype(jnp.bfloat16)
            return weight, jnp.exp2((old - new) * SCALE)

        def add(step, weight, factor):
            t, parts = step
            values = [
                kv[chunk, 1, at : at + HD, : min(HD, end - at)]
                for chunk, begin, end in parts for at in range(begin, end, HD)
            ]
            columns = jnp.concatenate(values, axis=1) if len(values) > 1 else values[0]
            columns = jnp.concatenate([columns, ones[:, : weight.shape[0]]], axis=0)
            acc[t] = acc[t] * factor[0:1] + jnp.dot(columns, weight, preferred_element_type=jnp.float32)

        score, before = scores(steps[0]), None
        for i, step in enumerate(steps):
            following = scores(steps[i + 1]) if i + 1 < len(steps) else None
            current = (step,) + weights(step, score)
            if before is not None:
                add(*before)
            before, score = current, following
            if i in between:
                between[i]()
        add(*before)

    def finish(t):
        total = acc[t]
        rows = (total[:HD] * (1.0 / total[HD : HD + 1])).T
        at = t * TILE
        while at < (t + 1) * TILE:
            block, row = at // QROWS, at % QROWS
            count = min(QROWS - row, (t + 1) * TILE - at)
            result[block, row : row + count, :] = rows[at - t * TILE : at - t * TILE + count]
            at += count

    def one_distance(distance, carry):
        lower, upper = lax.rem(z + PLANES - distance, PLANES), lax.rem(z + distance, PLANES)
        alone = (distance == 0) | (distance == 4)

        @pl.when(alone)
        def _():
            def late_first():
                pl.when(distance == 0)(lambda: pass_on(1, 1))

            def take_third():
                pl.when(distance == 4)(lambda: take_over(3))

            def last_first():
                pl.when(distance == 0)(lambda: pass_on(1, 2))

            def late_high():
                @pl.when(distance == 0)
                def _():
                    from_sibling(1, 2)

                @pl.when(distance == 4)
                def _():
                    pass_on(4, 2)
                    from_sibling(9, 2)

            attend(low(upper) + high(upper), {1: late_first, TILES - 3: late_high, TILES: last_first, TILES - 1: take_third})

        @pl.when((distance == 1) | (distance == 2))
        def _():
            def amid():
                pl.when(distance == 1)(lambda: pass_on(2, 0))
                pl.when(distance == 2)(lambda: pass_on(2, 2))

            def late():
                pl.when(distance == 2)(lambda: take_over(1))

            def last():
                pl.when(distance == 1)(lambda: pass_on(2, 1))
                pl.when(distance == 2)(lambda: pass_on(3, 0))

            from_sibling(2 * distance, 4)
            attend(low(lower, upper), {0: amid, 2: late, 3: last})

        @pl.when(distance == 3)
        def _():
            from_sibling(10, 2)
            so_far = steps((lower, 0, PIECE), (upper, PIECE, HALF))
            rest = steps((lower, PIECE, HALF), (upper, 0, PIECE))
            attend(
                so_far + rest,
                {
                    0: lambda: pass_on(3, 1),
                    TILES - 2: lambda: from_sibling(6, 2),
                    TILES - 1: lambda: pass_on(3, 2),
                    TILES + 1: lambda: take_over(2),
                    TILES + 2: lambda: pass_on(4, 0),
                },
            )

        @pl.when(distance > 1)
        def _():
            from_sibling(2 * distance - 1, 4)
            early = {t: lambda t=t: finish(t) for t in range(TILES) if SPAN[t][1] <= HALF}
            attend(high(lax.rem(lower + 1, PLANES), lax.rem(upper + PLANES - 1, PLANES)), early)
            pl.when(distance == 3)(lambda: from_sibling(8, 2))

        return carry

    lax.fori_loop(0, 5, one_distance, 0)

    for t in range(TILES):
        if SPAN[t][1] > HALF:
            finish(t)

    def out_copy(b, device_rows):
        return out.at[device_rows, :, pl.ds(pl.multiple_of(g * WIDE, HD), WIDE)]

    def send_back(group, carry):
        indices = [4 * group + 1 + j for j in range(4)]
        blocks = [lax.rem(me + i, BLOCKS) for i in indices]
        for b in blocks:
            rows = result[order[b]].astype(jnp.bfloat16)
            o_buf[b] = jnp.concatenate([rows[j * ROWS : (j + 1) * ROWS] for j in range(GROUP)], axis=1)
        for i, b in zip(indices, blocks):

            @pl.when(i < BLOCKS)
            def _():
                pltpu.make_async_remote_copy(
                    src_ref=o_buf.at[b], dst_ref=out_copy(b, part),
                    send_sem=o_send, recv_sem=o_recv,
                    device_id=plane_device(b), device_id_type=MESH,
                ).start()

        return carry

    lax.fori_loop(0, BLOCKS // 4, send_back, 0)
    own_o = pltpu.make_async_copy(o_buf.at[me], out_copy(me, part), o_own)
    own_o.start()

    many_o = o_buf.at[pl.ds(0, 31)]
    pltpu.make_async_copy(many_q, many_q, q_send).wait()
    pltpu.make_async_copy(many, many, kv_send).wait()
    for distance in range(1, 5):
        for turn in range(0, TURNS, 1 if distance < 4 else 2):
            ring(distance, True, turn).wait_send()
            ring(distance, False, turn).wait_send()
        if distance < 4:
            over(distance, z, 0, 2).wait_send()
    for step in range(11):
        across(step, z, 0, 4 if step in (2, 3, 4, 5, 7) else 2).wait_send()
    own_o.wait()
    pltpu.make_async_copy(many_o, many_o, o_send).wait()
    pltpu.make_async_copy(many_o, many_o, o_recv).wait()


def shards(queries, keys, values, order):
    hbm = pl.BlockSpec(memory_space=pltpu.HBM)
    dma = pltpu.SemaphoreType.DMA
    out = pl.pallas_call(
        kernel,
        out_shape=pltpu.VMEM((PART // ROWS, ROWS, 8 * WIDE), jnp.bfloat16),
        in_specs=[pl.BlockSpec(memory_space=pltpu.SMEM), hbm, hbm, hbm],
        out_specs=pl.BlockSpec(memory_space=pltpu.VMEM),
        scratch_shapes=[
            pltpu.VMEM((PART // ROWS, ROWS, 8 * WIDE), jnp.bfloat16),
            pltpu.VMEM((2, PART, 8 * HD), jnp.bfloat16),
            pltpu.VMEM((2, 8, PART, HD), jnp.bfloat16),
            pltpu.VMEM((BLOCKS, ROWS, WIDE), jnp.bfloat16),
            pltpu.VMEM((BLOCKS, PART, HD), jnp.bfloat16),
            pltpu.VMEM((PLANES, 2, CHUNK, HD), jnp.bfloat16),
            pltpu.VMEM((QALL, HD), jnp.bfloat16),
            pltpu.VMEM((VROWS - HD, CHUNK), jnp.bfloat16),
            pltpu.VMEM((TILES, VROWS, TILE), jnp.float32),
            pltpu.VMEM((TILES, 8, TILE), jnp.float32),
            pltpu.VMEM((3, TILES, EDGE, TILE), jnp.float32),
            pltpu.VMEM((BLOCKS, QROWS, HD), jnp.float32),
            pltpu.VMEM((BLOCKS, ROWS, WIDE), jnp.bfloat16),
            pltpu.SMEM((BLOCKS,), jnp.int32),
            dma((3,)), dma, dma, dma, dma, dma, dma,
            *[dma((4 * TURNS,))] * 4, dma((11,)), dma((11,)), dma((3,)), dma((3,)),
            dma, dma, dma,
        ],
        compiler_params=pltpu.CompilerParams(
            collective_id=0, has_side_effects=True, vmem_limit_bytes=60 * 2**20
        ),
        cost_estimate=pl.CostEstimate(
            flops=4 * QALL * BLOCKS * BLK * HD // 2, bytes_accessed=2**21, transcendentals=QALL * 4096
        ),
    )(order, queries.reshape(PART // ROWS, ROWS, 8 * WIDE), keys, values)
    return out.reshape(PART, 8 * WIDE)


def solution(mesh):
    rows = P(("ctx", "head"), None)
    return jax.shard_map(
        shards, mesh=mesh, in_specs=(rows, rows, rows, P()), out_specs=rows, check_vma=False
    )
```
